32 devices in a mesh: rep: 2 (over x), cols: 8 (over z, y), blk: 2 (over core).
Axes of the slice: x: 2, y: 2, z: 4, core: 2. Of those that a mesh axis runs over, the one named last changes fastest.
Arguments:
- acts: bfloat16 [4096, 3584], P(('rep', 'blk'), 'cols'), parts along dimension 0, may hold values from -6 to 6
- grads: bfloat16 [4096, 14336], P(('rep', 'blk'), 'cols'), parts along dimension 0, may hold values from -6 to 6
- eigvecs: bfloat16 [4, 3584, 14336], P('blk', None, 'cols'), may hold values from -0.0008544922 to 0.0008544922
- seg_ids: int32 [4096], P(('rep', 'blk')), parts along dimension 0, may hold values from 0 to 15, never falling along the last dimension, each value on 1 to 256 neighbouring positions
- keep: int32 [4096], P(('rep', 'blk')), parts along dimension 0, may hold values 0 or 1
- queries: float32 [32, 4], P('rep'), parts along dimension 0, may hold values from -6 to 6
- eigvals: float32 [4], replicated, may hold values from 0.25 to 4
Outputs:
- scores: float32 [4, 32], P(None, 'rep'), parts along dimension 1
- influence: float32 [16, 32], P(None, 'rep'), parts along dimension 1
The draws below stay inside these ranges and needn't reach their ends.
There are 2 independent parts, one for each index of `rep`. The reference program is written for one: setup_inputs(seed, part) draws one part's arguments, and reference() takes and returns one part's arrays. A program takes and returns all parts, laid end to end along the dimension named above; an argument that names none is the same for every part. Nothing has to cross between parts.
Inputs may be any that keep to these rules, and one draw needn't show every extreme that they name: `seg_ids`: segment numbers never fall along the tokens; each sequence has 1 to 256 tokens.
All inputs are finite; a program needn't handle non-finite values. No bound on the sum of `keep` on one device may be relied on, other than what follows from the above.
Results may differ from the reference program's by a relative error of at most 0.0003.
Values may be sent and summed in bfloat16 or wider, within the bound.
A program may use at most 192 MiB of HBM per device.

```python
import math
import jax
import jax.numpy as jnp
import numpy as np
from jax import lax

D = 3584
FF = 14336
NSEG = 16
QUERIES = 16
K = 4
TOKENS = 2048
SEG_MOST = 256


def place_ends(drawn, rng, least, high):
    place = [jax.random.randint(jax.random.fold_in(rng, axis), (), 0, length) for axis, length in enumerate(drawn.shape)]
    widest = drawn.shape.index(max(drawn.shape))
    next_to = place[:widest] + [(place[widest] + 1) % drawn.shape[widest]] + place[widest + 1:]
    return drawn.at[tuple(place)].set(least).at[tuple(next_to)].set(high)


def shard_levels(stream_key, dims, shards, least, largest):
    gain = 1.0
    for position, blocks in shards:
        draws = jax.random.uniform(jax.random.fold_in(jax.random.fold_in(stream_key, 6), position), (blocks,), jnp.float32, least / len(shards), largest / len(shards))
        gain = gain * jnp.repeat(jnp.exp(draws), dims[position] // blocks).reshape((-1,) + (1,) * (len(dims) - 1 - position))
    return gain


def split_up(number_of, total, limit, lean):
    loads = [(1 << 20) // math.isqrt(rank ** lean) + 1 for rank in range(2, number_of + 1)]
    rest, counts = total - limit - (number_of - 1), [1] * (number_of - 1)
    while rest > 0:
        candidates = [i for i in range(number_of - 1) if counts[i] < limit]
        whole, left = sum([loads[i] for i in candidates]), rest
        for i in candidates:
            more = min(limit - counts[i], max(1, left * loads[i] // whole), rest)
            counts[i] = counts[i] + more
            rest = rest - more
    return np.array([limit] + counts)


def ragged_sizes(stream_key, amount, total, bound, slope):
    if amount == 2:
        one = jax.random.randint(stream_key, (), max(1, total - bound), min(bound, total - 1) + 1)
        return jnp.stack([one, total - one])
    lengths = jnp.asarray(split_up(amount, total, bound, slope), jnp.int32)
    pairs = (amount - 1) // 2
    donor, taker = lengths[1:1 + 2 * pairs:2], lengths[2:2 + 2 * pairs:2]
    margin = jnp.minimum(donor - 1, bound - taker)
    shifted = jax.random.randint(jax.random.fold_in(stream_key, 1), (pairs,), 0, 1 << 20) % (margin + 1)
    lengths = lengths.at[1:1 + 2 * pairs:2].set(donor - shifted).at[2:2 + 2 * pairs:2].set(taker + shifted)
    return lengths[jax.random.permutation(jax.random.fold_in(stream_key, 2), amount)]


def noise(key, shape, deviation, most, cuts=(), held_as=jnp.bfloat16):
    entries = jax.random.normal(key, shape, jnp.float32) * deviation
    if len(cuts) > 0:
        entries = shard_levels(key, shape, cuts, -0.22, 0.18) * entries
    return jnp.clip(entries, min=-most, max=most).astype(held_as)


def setup_inputs(seed: int = 0, part: int = 0) -> dict:
    keys = jax.random.split(jax.random.key(seed), 8)
    part_keys = jax.random.split(jax.random.fold_in(keys[7], part), 8)
    acts = noise(part_keys[0], (TOKENS, D), 1.0, 6.0, ((0, 2), (1, 8)))
    grads = noise(part_keys[1], (TOKENS, FF), 1.0, 6.0, ((0, 2), (1, 8)))
    eigvecs = noise(keys[2], (K, D, FF), (D * FF) ** -0.5, 0.0008544922, ((0, 2), (2, 8)))
    seg_ids = jnp.searchsorted(jnp.cumsum(ragged_sizes(part_keys[3], NSEG, TOKENS, SEG_MOST, 1)), jnp.arange(TOKENS), side="right").astype(jnp.int32)
    keep = place_ends((jax.random.randint(part_keys[4], (TOKENS,), 0, 4) < 3).astype(jnp.int32), jax.random.fold_in(part_keys[4], 1), 0, 1)
    queries = noise(part_keys[5], (QUERIES, K), 1.0, 6.0, (), jnp.float32)
    eigvals = jnp.clip(jnp.exp(jax.random.uniform(keys[6], (K,), jnp.float32, math.log(0.25), math.log(4.0))), 0.25, 4.0)
    return dict(acts=acts, grads=grads, eigvecs=eigvecs, seg_ids=seg_ids, keep=keep, queries=queries, eigvals=eigvals)


def reference(acts, grads, eigvecs, seg_ids, keep, queries, eigvals):
    grad_float = grads.astype(jnp.float32)

    def one_vector(weight):
        proj = jnp.dot(acts, weight, preferred_element_type=jnp.float32)
        return lax.optimization_barrier(jnp.sum(proj * grad_float, axis=1))
    terms = lax.map(one_vector, eigvecs)
    member = ((seg_ids[:, None] == jnp.arange(NSEG, dtype=jnp.int32)[None, :]) & (keep[:, None] == 1)).astype(jnp.float32)
    sums = jnp.dot(terms, member, precision=lax.Precision.HIGHEST)
    scores = sums * jnp.float32(1.0 / math.sqrt(SEG_MOST))
    weighted = queries / eigvals[None, :]
    influence = jnp.dot(weighted, scores, precision=lax.Precision.HIGHEST)
    return (scores, influence)
```

```python
import functools
import math

import jax
import jax.numpy as jnp
from jax import lax
from jax.experimental import pallas as pl
from jax.experimental.pallas import tpu as pltpu
from jax.sharding import PartitionSpec as P

NSEG = 16
MESH = pl.DeviceIdType.MESH
UP, DOWN, ACROSS, SIB = range(4)


def nearest(nz):
    return [sorted(range(nz), key=lambda o: (abs(o - z), o)) for z in range(nz)]


def kernel(ny, nz, tile, a_ref, g_ref, code_ref, e_ref, out_ref, acts, grads, codes, ebuf, acc, red,
           send, recv, own_sem, e_sem, g_send, g_recv, c_send, c_recv, r_send, r_recv):
    n = ny * nz
    rows, tokens = a_ref.shape
    kk = e_ref.shape[0]
    core = lax.axis_index("blk")
    other = 1 - core
    me = lax.axis_index("cols")
    z, y = me // ny, me % ny
    table = nearest(nz)
    order = []
    for i in range(nz):
        pick = jnp.int32(0)
        for zz in range(nz):
            pick = pick + jnp.where(z == zz, jnp.int32(table[zz][i]), jnp.int32(0))
        order.append(pick)

    barrier = pltpu.get_barrier_semaphore()
    for i in range(1, n):
        pl.semaphore_signal(barrier, inc=1, device_id={"cols": lax.rem(me + i, n)}, device_id_type=MESH)
    pl.semaphore_signal(barrier, inc=1, device_id={"blk": other}, device_id_type=MESH)
    pl.semaphore_wait(barrier, n)

    def move(j, kind, first):
        src = a_ref if first else acts.at[j, core]
        dest = {UP: {"cols": me + ny}, DOWN: {"cols": me - ny}, ACROSS: {"cols": z * ny + (1 - y)}, SIB: {"blk": other}}[kind]
        return pltpu.make_async_remote_copy(
            src_ref=src, dst_ref=acts.at[j, core], send_sem=send.at[j, kind], recv_sem=recv.at[j, core],
            device_id=dest, device_id_type=MESH)

    def arrived(j, c):
        pltpu.make_async_remote_copy(
            src_ref=acts.at[j, c], dst_ref=acts.at[j, c], send_sem=send.at[j, SIB], recv_sem=recv.at[j, c],
            device_id={"blk": other}, device_id_type=MESH).wait_recv()

    def load(p, j):
        return pltpu.make_async_copy(e_ref.at[:, pl.ds(pl.multiple_of(j * rows, 16), rows), :], ebuf.at[p % 2], e_sem.at[p % 2])

    def gswap():
        return pltpu.make_async_remote_copy(src_ref=g_ref, dst_ref=grads.at[core], send_sem=g_send, recv_sem=g_recv,
                                            device_id={"blk": other}, device_id_type=MESH)

    def cswap():
        return pltpu.make_async_remote_copy(src_ref=code_ref, dst_ref=codes.at[core], send_sem=c_send, recv_sem=c_recv,
                                            device_id={"blk": other}, device_id_type=MESH)

    own = [pltpu.make_async_copy(a_ref, acts.at[me, core], own_sem.at[0]),
           pltpu.make_async_copy(g_ref, grads.at[core], own_sem.at[1]),
           pltpu.make_async_copy(code_ref, codes.at[core], own_sem.at[2])]

    @pl.when(z < nz - 1)
    def _():
        move(me, UP, True).start()

    @pl.when(z > 0)
    def _():
        move(me, DOWN, True).start()

    if ny > 1:
        move(me, ACROSS, True).start()
    move(me, SIB, True).start()
    for copy in own:
        copy.start()
    gswap().start()
    cswap().start()

    seq = [(0, 0)]
    for i in range(1, nz):
        seq.append((i, 0))
        if ny > 1:
            seq.append((i - 1, 1))
    if ny > 1:
        seq.append((nz - 1, 1))

    def chunk(item):
        i, far = item
        return order[i] * ny + ((1 - y) if far else y)

    load(0, chunk(seq[0])).start()
    acc[...] = jnp.zeros_like(acc)
    for copy in own:
        copy.wait()

    def compute(p, j, c):
        @pl.loop(0, tokens // tile)
        def _(t):
            cols = pl.ds(pl.multiple_of(t * tile, tile), tile)
            g = grads[c, :, cols]
            a = acts[j, c, :, cols].astype(jnp.float32)
            for k in range(kk):
                q = jnp.dot(ebuf[p % 2, k], g, preferred_element_type=jnp.float32)
                acc[k, c, :, cols] += jnp.sum((q * a).reshape(rows // 8, 8, tile), axis=0)

    def hop(h):
        @pl.when(z - h >= 0)
        def _():
            j = me - h * ny
            arrived(j, core)

            @pl.when(z < nz - 1)
            def _():
                move(j, UP, False).start()
            if ny > 1:
                move(j, ACROSS, False).start()
            move(j, SIB, False).start()

        @pl.when(z + h <= nz - 1)
        def _():
            j = me + h * ny
            arrived(j, core)

            @pl.when(z > 0)
            def _():
                move(j, DOWN, False).start()
            if ny > 1:
                move(j, ACROSS, False).start()
            move(j, SIB, False).start()

    for p, item in enumerate(seq):
        i, far = item
        j = chunk(item)
        if i > 0 and not far:
            hop(i)
        if far:
            arrived(j, core)
            move(j, SIB, False).start()
        if p + 1 < n:
            load(p + 1, chunk(seq[p + 1])).start()
        load(p, j).wait()
        compute(p, j, core)
        if p == 0:
            gswap().wait_recv()
        arrived(j, other)
        compute(p, j, other)

    cswap().wait_recv()
    lane = lax.broadcasted_iota(jnp.int32, (8, 128), 1)
    row = lax.broadcasted_iota(jnp.int32, (8, 128), 0)
    part = jnp.zeros((8, 128), jnp.float32)
    for k in range(kk):
        for s in range(NSEG):
            tot = jnp.zeros((8, 128), jnp.float32)
            for c in range(2):
                hit = jnp.where(codes[c] == s, acc[k, c], 0.0)
                for b in range(tokens // 128):
                    tot = tot + hit[:, b * 128:(b + 1) * 128]
            val = jnp.sum(jnp.sum(tot, axis=0, keepdims=True), axis=1, keepdims=True)
            part = part + jnp.where((lane == s) & (row == k), jnp.broadcast_to(val, (8, 128)), 0.0)
    bits = n.bit_length() - 1

    def share(b):
        if b < bits:
            size = 1 << b
            up = (me // size) % 2
            dest = {"cols": me + size - 2 * size * up}
        else:
            dest = {"blk": other}
        return pltpu.make_async_remote_copy(src_ref=red.at[b, 0], dst_ref=red.at[b, 1], send_sem=r_send.at[b],
                                            recv_sem=r_recv.at[b], device_id=dest, device_id_type=MESH)

    for b in range(bits):
        red[b, 0] = part
        share(b).start()
        share(b).wait_recv()
        part = part + red[b, 1]
    red[bits, 0] = part
    share(bits).start()
    share(bits).wait_recv()
    theirs = red[bits, 1]
    out_ref[0] = jnp.where(core == 0, part, theirs)
    out_ref[1] = jnp.where(core == 0, theirs, part)

    for b in range(bits + 1):
        share(b).wait_send()
    gswap().wait_send()
    cswap().wait_send()

    for i in range(nz):
        j = order[i] * ny + y
        first = i == 0

        @pl.when((order[i] <= z) & (z < nz - 1))
        def _():
            move(j, UP, first).wait_send()

        @pl.when((order[i] >= z) & (z > 0))
        def _():
            move(j, DOWN, first).wait_send()
        if ny > 1:
            move(j, ACROSS, first).wait_send()
            move(order[i] * ny + (1 - y), SIB, False).wait_send()
        move(j, SIB, first).wait_send()


def fused(n, at, gt, code, eigvecs):
    ny = 2 if n == 8 else 1
    nz = n // ny
    rows, tokens = at.shape
    width = gt.shape[0]
    kk = eigvecs.shape[0]
    bits = n.bit_length() - 1
    any_spec = pl.BlockSpec(memory_space=pl.ANY)
    dma = pltpu.SemaphoreType.DMA
    return pl.pallas_call(
        functools.partial(kernel, ny, nz, math.gcd(tokens, 512)),
        out_shape=jax.ShapeDtypeStruct((2, 8, 128), jnp.float32),
        in_specs=[any_spec, any_spec, any_spec, any_spec],
        out_specs=pl.BlockSpec(memory_space=pltpu.VMEM),
        scratch_shapes=[
            pltpu.VMEM((n, 2, rows, tokens), jnp.bfloat16),
            pltpu.VMEM((2, width, tokens), jnp.bfloat16),
            pltpu.VMEM((2, 8, tokens), jnp.int32),
            pltpu.VMEM((2, kk, rows, width), jnp.bfloat16),
            pltpu.VMEM((kk, 2, 8, tokens), jnp.float32),
            pltpu.VMEM((bits + 1, 2, 8, 128), jnp.float32),
            dma((n, 4)), dma((n, 2)), dma((3,)), dma((2,)), dma, dma, dma, dma,
            dma((bits + 1,)), dma((bits + 1,)),
        ],
        compiler_params=pltpu.CompilerParams(collective_id=0, has_side_effects=True, vmem_limit_bytes=58 * 1024 * 1024),
        cost_estimate=pl.CostEstimate(flops=2 * n * rows * 2 * tokens * width * kk, bytes_accessed=eigvecs.size * 2, transcendentals=0),
    )(at, gt, code, eigvecs)


def local(n, acts, grads, eigvecs, seg_ids, keep, queries, eigvals):
    kk = eigvecs.shape[0]
    seg_most = acts.shape[0] * 2 // 8
    code = jnp.where(keep == 1, seg_ids, jnp.int32(-1))
    code = jnp.broadcast_to(code[None, :], (8, code.shape[0]))
    out = fused(n, acts.T, grads.T, code, eigvecs)
    sums = out[:, :kk, :NSEG].reshape(2 * kk, NSEG)
    scores = sums * jnp.float32(1.0 / math.sqrt(seg_most))
    weighted = queries / eigvals[None, :]
    influence = jnp.dot(weighted, scores, precision=lax.Precision.HIGHEST)
    return (scores, influence)


def solution(mesh):
    placed = (
        P(("rep", "blk"), "cols"),
        P(("rep", "blk"), "cols"),
        P("blk", None, "cols"),
        P(("rep", "blk")),
        P(("rep", "blk")),
        P("rep", None),
        P(),
    )
    return jax.shard_map(
        functools.partial(local, mesh.shape["cols"]),
        mesh=mesh,
        in_specs=placed,
        out_specs=(P(None, "rep"), P(None, "rep")),
        check_vma=False,
    )
```

```python
import functools
import math

import jax
import jax.numpy as jnp
from jax import lax
from jax.experimental import pallas as pl
from jax.experimental.pallas import tpu as pltpu
from jax.sharding import PartitionSpec as P

NSEG = 16
MESH = pl.DeviceIdType.MESH
UP, DOWN, ACROSS, SIB = range(4)


def nearest(nz):
    return [sorted(range(nz), key=lambda o: (abs(o - z), o)) for z in range(nz)]


def kernel(ny, nz, tile, scale, a_ref, g_ref, e_ref, seg_ref, keep_ref, q_ref, v_ref, scores_ref, inf_ref, acts, grads, codes, ebuf, acc, red,
           send, recv, small_send, small_recv, own_sem, e_sem, g_send, g_recv, c_send, c_recv, r_send, r_recv):
    n = ny * nz
    rows, tokens = a_ref.shape
    kk = e_ref.shape[0]
    small = 128 if ny > 1 else 0
    large = tokens - small
    core = lax.axis_index("blk")
    other = 1 - core
    me = lax.axis_index("cols")
    z, y = me // ny, me % ny
    table = nearest(nz)
    order = []
    for i in range(nz):
        pick = jnp.int32(0)
        for zz in range(nz):
            pick = pick + jnp.where(z == zz, jnp.int32(table[zz][i]), jnp.int32(0))
        order.append(pick)

    barrier = pltpu.get_barrier_semaphore()
    for i in range(1, n):
        pl.semaphore_signal(barrier, inc=1, device_id={"cols": lax.rem(me + i, n)}, device_id_type=MESH)
    pl.semaphore_signal(barrier, inc=1, device_id={"blk": other}, device_id_type=MESH)
    pl.semaphore_wait(barrier, n)

    spans = (pl.ds(0, large), pl.ds(large, small))
    sends, recvs = (send, small_send), (recv, small_recv)

    def move(j, kind, first, piece=0):
        if first:
            src = a_ref.at[:, spans[piece]]
        else:
            src = acts.at[j, core, :, spans[piece]]
        dest = {UP: {"cols": me + ny}, DOWN: {"cols": me - ny}, ACROSS: {"cols": z * ny + (1 - y)}, SIB: {"blk": other}}[kind]
        return pltpu.make_async_remote_copy(
            src_ref=src, dst_ref=acts.at[j, core, :, spans[piece]], send_sem=sends[piece].at[j, kind],
            recv_sem=recvs[piece].at[j, core], device_id=dest, device_id_type=MESH)

    def arrived(j, c, piece=0):
        ref = acts.at[j, c, :, spans[piece]]
        pltpu.make_async_remote_copy(
            src_ref=ref, dst_ref=ref, send_sem=sends[piece].at[j, SIB], recv_sem=recvs[piece].at[j, c],
            device_id={"blk": other}, device_id_type=MESH).wait_recv()

    def load(p, j):
        return pltpu.make_async_copy(e_ref.at[:, pl.ds(pl.multiple_of(j * rows, 16), rows), :], ebuf.at[p % 2], e_sem.at[p % 2])

    def gswap():
        return pltpu.make_async_remote_copy(src_ref=g_ref, dst_ref=grads.at[core], send_sem=g_send, recv_sem=g_recv,
                                            device_id={"blk": other}, device_id_type=MESH)

    def cswap():
        return pltpu.make_async_remote_copy(src_ref=codes.at[core], dst_ref=codes.at[core], send_sem=c_send, recv_sem=c_recv,
                                            device_id={"blk": other}, device_id_type=MESH)

    own = [pltpu.make_async_copy(a_ref, acts.at[me, core], own_sem.at[0]),
           pltpu.make_async_copy(g_ref, grads.at[core], own_sem.at[1])]

    if small:
        move(me, ACROSS, True, 1).start()

    @pl.when(z < nz - 1)
    def _():
        move(me, UP, True).start()

    @pl.when(z > 0)
    def _():
        move(me, DOWN, True).start()

    if ny > 1:
        move(me, ACROSS, True).start()
    if small:
        @pl.when(z < nz - 1)
        def _():
            move(me, UP, True, 1).start()

        @pl.when(z > 0)
        def _():
            move(me, DOWN, True, 1).start()

        move(me, SIB, True, 1).start()
    move(me, SIB, True).start()
    for copy in own:
        copy.start()
    gswap().start()
    codes[core] = jnp.where(keep_ref[...] == 1, seg_ref[...], jnp.int32(-1))
    cswap().start()

    seq = [(0, 0)]
    for i in range(1, nz):
        seq.append((i, 0))
        if ny > 1:
            seq.append((i - 1, 1))
    if ny > 1:
        seq.append((nz - 1, 1))

    def chunk(item):
        i, far = item
        return order[i] * ny + ((1 - y) if far else y)

    load(0, chunk(seq[0])).start()
    acc[...] = jnp.zeros_like(acc)
    for copy in own:
        copy.wait()

    def compute(p, j, c):
        @pl.loop(0, tokens // tile)
        def _(t):
            cols = pl.ds(pl.multiple_of(t * tile, tile), tile)
            g = grads[c, cols, :]
            a = acts[j, c, :, cols].astype(jnp.float32)
            for k in range(kk):
                q = lax.dot_general(ebuf[p % 2, k], g, (((1,), (1,)), ((), ())), preferred_element_type=jnp.float32)
                acc[k, c, :, cols] += jnp.sum((q * a).reshape(rows // 8, 8, tile), axis=0)

    def hop(h):
        @pl.when(z - h >= 0)
        def _():
            j = me - h * ny
            arrived(j, core)

            @pl.when(z < nz - 1)
            def _():
                move(j, UP, False).start()
            if ny > 1:
                move(j, ACROSS, False).start()
            move(j, SIB, False).start()

        @pl.when(z + h <= nz - 1)
        def _():
            j = me + h * ny
            arrived(j, core)

            @pl.when(z > 0)
            def _():
                move(j, DOWN, False).start()
            if ny > 1:
                move(j, ACROSS, False).start()
            move(j, SIB, False).start()

    def small_pass(j, up, down):
        arrived(j, core, 1)
        if up:
            @pl.when(z < nz - 1)
            def _():
                move(j, UP, False, 1).start()
        if down:
            @pl.when(z > 0)
            def _():
                move(j, DOWN, False, 1).start()
        move(j, SIB, False, 1).start()

    def small_hop(h, far):
        shift = (1 - 2 * y) if far else 0

        @pl.when(z - h >= 0)
        def _():
            small_pass(me - h * ny + shift, True, False)

        @pl.when(z + h <= nz - 1)
        def _():
            small_pass(me + h * ny + shift, False, True)

    for p, item in enumerate(seq):
        i, far = item
        j = chunk(item)
        if i > 0 and not far:
            hop(i)
            if small:
                small_hop(i, False)
        if far:
            arrived(j, core)
            move(j, SIB, False).start()
        if p + 1 < n:
            load(p + 1, chunk(seq[p + 1])).start()
        load(p, j).wait()
        compute(p, j, core)
        if p == 0:
            if small:
                small_pass(z * ny + (1 - y), True, True)
            gswap().wait_recv()
        elif small and not far:
            small_hop(i, True)
        arrived(j, other)
        if small:
            arrived(j, other, 1)
        compute(p, j, other)

    cswap().wait_recv()
    lane = lax.broadcasted_iota(jnp.int32, (8, 128), 1)
    row = lax.broadcasted_iota(jnp.int32, (8, 128), 0)
    part = jnp.zeros((8, 128), jnp.float32)
    for k in range(kk):
        for s in range(NSEG):
            tot = jnp.zeros((8, 128), jnp.float32)
            for c in range(2):
                for b in range(tokens // 128):
                    tot = tot + jnp.where(codes[c, b:b + 1, :] == s, acc[k, c, :, b * 128:(b + 1) * 128], 0.0)
            val = jnp.sum(jnp.sum(tot, axis=0, keepdims=True), axis=1, keepdims=True)
            part = part + jnp.where((lane == s) & (row == k), jnp.broadcast_to(val, (8, 128)), 0.0)
    bits = n.bit_length() - 1

    def share(b):
        if b < bits:
            size = 1 << b
            up = (me // size) % 2
            dest = {"cols": me + size - 2 * size * up}
        else:
            dest = {"blk": other}
        return pltpu.make_async_remote_copy(src_ref=red.at[b, 0], dst_ref=red.at[b, 1], send_sem=r_send.at[b],
                                            recv_sem=r_recv.at[b], device_id=dest, device_id_type=MESH)

    for b in range(bits):
        red[b, 0] = part
        share(b).start()
        share(b).wait_recv()
        part = part + red[b, 1]
    red[bits, 0] = part
    share(bits).start()
    share(bits).wait_recv()
    theirs = red[bits, 1]
    halves = (jnp.where(core == 0, part, theirs), jnp.where(core == 0, theirs, part))
    weighted = q_ref[...] / v_ref[...]
    total = jnp.zeros(inf_ref.shape, jnp.float32)
    for c in range(2):
        for k in range(kk):
            line = halves[c][k:k + 1, :NSEG] * scale
            scores_ref[c * kk + k:c * kk + k + 1, :] = line
            total = total + weighted[:, c * kk + k:c * kk + k + 1] * line
    inf_ref[...] = total

    for b in range(bits + 1):
        share(b).wait_send()
    gswap().wait_send()
    cswap().wait_send()

    for i in range(nz):
        j = order[i] * ny + y
        first = i == 0

        @pl.when((order[i] <= z) & (z < nz - 1))
        def _():
            move(j, UP, first).wait_send()

        @pl.when((order[i] >= z) & (z > 0))
        def _():
            move(j, DOWN, first).wait_send()
        if ny > 1:
            move(j, ACROSS, first).wait_send()
            move(order[i] * ny + (1 - y), SIB, False).wait_send()
        move(j, SIB, first).wait_send()
        if small:
            f = order[i] * ny + (1 - y)

            @pl.when((order[i] <= z) & (z < nz - 1))
            def _():
                move(j, UP, first, 1).wait_send()
                move(f, UP, False, 1).wait_send()

            @pl.when((order[i] >= z) & (z > 0))
            def _():
                move(j, DOWN, first, 1).wait_send()
                move(f, DOWN, False, 1).wait_send()
            if first:
                move(j, ACROSS, first, 1).wait_send()
            move(j, SIB, first, 1).wait_send()
            move(f, SIB, False, 1).wait_send()


def local(n, acts, grads, eigvecs, seg_ids, keep, queries, eigvals):
    ny = 2 if n == 8 else 1
    nz = n // ny
    tokens, rows = acts.shape
    width = grads.shape[1]
    kk = eigvecs.shape[0]
    bits = n.bit_length() - 1
    any_spec = pl.BlockSpec(memory_space=pl.ANY)
    vmem = pl.BlockSpec(memory_space=pltpu.VMEM)
    dma = pltpu.SemaphoreType.DMA
    scale = 1.0 / math.sqrt(tokens * 2 // 8)
    return pl.pallas_call(
        functools.partial(kernel, ny, nz, math.gcd(tokens, 512), scale),
        out_shape=(jax.ShapeDtypeStruct((2 * kk, NSEG), jnp.float32),
                   jax.ShapeDtypeStruct((queries.shape[0], NSEG), jnp.float32)),
        in_specs=[any_spec] * 3 + [vmem] * 4,
        out_specs=(vmem, vmem),
        scratch_shapes=[
            pltpu.VMEM((n, 2, rows, tokens), jnp.bfloat16),
            pltpu.VMEM((2, tokens, width), jnp.bfloat16),
            pltpu.VMEM((2, tokens // 128, 128), jnp.int32),
            pltpu.VMEM((2, kk, rows, width), jnp.bfloat16),
            pltpu.VMEM((kk, 2, 8, tokens), jnp.float32),
            pltpu.VMEM((bits + 1, 2, 8, 128), jnp.float32),
            dma((n, 4)), dma((n, 2)), dma((n, 4)), dma((n, 2)), dma((2,)), dma((2,)), dma, dma, dma, dma,
            dma((bits + 1,)), dma((bits + 1,)),
        ],
        compiler_params=pltpu.CompilerParams(collective_id=0, has_side_effects=True, vmem_limit_bytes=58 * 1024 * 1024),
        cost_estimate=pl.CostEstimate(flops=2 * n * rows * 2 * tokens * width * kk, bytes_accessed=eigvecs.size * 2, transcendentals=0),
    )(acts.T, grads, eigvecs, seg_ids.reshape(-1, 128), keep.reshape(-1, 128), queries, eigvals[None, :])


def solution(mesh):
    placed = (
        P(("rep", "blk"), "cols"),
        P(("rep", "blk"), "cols"),
        P("blk", None, "cols"),
        P(("rep", "blk")),
        P(("rep", "blk")),
        P("rep", None),
        P(),
    )
    return jax.shard_map(
        functools.partial(local, mesh.shape["cols"]),
        mesh=mesh,
        in_specs=placed,
        out_specs=(P(None, "rep"), P(None, "rep")),
        check_vma=False,
    )
```
